32 devices in a mesh: dp: 8 (over y, x, core), seq: 4 (over z).
Axes of the slice: x: 2, y: 2, z: 4, core: 2. Of those that a mesh axis runs over, the one named last changes fastest.
Arguments:
- queries: bfloat16 [8192, 1536], P(('dp', 'seq')), may hold values from -8 to 8
- keys: bfloat16 [8192, 1536], P(('dp', 'seq')), may hold values from -8 to 8
- values: bfloat16 [8192, 1536], P(('dp', 'seq')), may hold values from -6 to 6
- grad_out: bfloat16 [8192, 3072], P(('dp', 'seq')), may hold values from -2 to 2
- out_weight: bfloat16 [3072, 1536], P('dp', 'seq'), may hold values from -0.15625 to 0.15625
- clip_lengths: int32 [8, 3], P('dp'), may hold values from 1 to 512, 1024 in all within a row
Outputs:
- grad_queries: bfloat16 [8192, 1536], P(('dp', 'seq'))
- grad_keys: bfloat16 [8192, 1536], P(('dp', 'seq'))
- grad_values: bfloat16 [8192, 1536], P(('dp', 'seq'))
- grad_weight: float32 [3072, 1536], P('dp', 'seq')
The draws below stay inside these ranges and needn't reach their ends.
Inputs may be any that keep to these rules, and one draw needn't show every extreme that they name: `clip_lengths`: each row holds 3 lengths that sum to 1024; the largest of each row is exactly 512.
All inputs are finite; a program needn't handle non-finite values.
Results may differ from the reference program's by a relative error of at most 0.012.
The reference program's roundings to bfloat16 on the way (of `grad_attention`, `probs_low`, `attention` and `grad_scores`) count: a program that leaves them out, or rounds other values in their place, can miss the bound.
Values may be sent and summed in bfloat16 or wider, within the bound.
A program may use at most 128 MiB of HBM per device.

```python
import math
import jax
import jax.numpy as jnp
import numpy as np
from jax import lax

D = 3072
HEADS = 12
HEAD_DIM = 128
TOK_DEV = 256
CLIPS = 3
HD = 1536
TOKENS = 8192
N_DP = 8
N_SEQ = 4


def draw_queries(key, part):
    key = jax.random.fold_in(key, 101)
    base = jnp.clip(jax.random.normal(key, (TOKENS, HD), jnp.float32), -6.0, 6.0)
    return base.astype(jnp.bfloat16)


def draw_keys(key, part):
    key = jax.random.fold_in(key, 202)
    base = jnp.clip(jax.random.normal(key, (TOKENS, HD), jnp.float32), -6.0, 6.0)
    return base.astype(jnp.bfloat16)


def raised(drawn, stream_key, source, target, blocks, factor):
    owner, partner = [(jnp.arange(drawn.shape[dim]) // (drawn.shape[dim] // blocks)).reshape([-1 if axis == dim else 1 for axis in range(drawn.ndim)]) for dim in (source, target)]
    chosen = jax.random.permutation(stream_key, blocks)[partner]
    strong = (owner == chosen) | (owner == (partner + blocks // 2) % blocks)
    return jnp.where(strong, factor * drawn, drawn)


def shard_levels(rng, extent, cuts, least, largest):
    level = 1.0
    for position, blocks in cuts:
        draws = jax.random.uniform(jax.random.fold_in(jax.random.fold_in(rng, 6), position), (blocks,), jnp.float32, least / len(cuts), largest / len(cuts))
        level = level * jnp.repeat(jnp.exp(draws), extent[position] // blocks).reshape((-1,) + (1,) * (len(extent) - 1 - position))
    return level


def profile(count, total, limit, lean):
    weights = [(1 << 20) // math.isqrt(standing ** lean) + 1 for standing in range(2, count + 1)]
    surplus, given = total - limit - (count - 1), [1] * (count - 1)
    while surplus > 0:
        movable = [i for i in range(count - 1) if given[i] < limit]
        pool, budget = sum([weights[i] for i in movable]), surplus
        for i in movable:
            more = min(limit - given[i], max(1, budget * weights[i] // pool), surplus)
            given[i] = given[i] + more
            surplus = surplus - more
    return np.array([limit] + given)


def ragged(own_key, count, total, limit, skew):
    if count == 2:
        one = jax.random.randint(own_key, (), max(1, total - limit), min(limit, total - 1) + 1)
        return jnp.stack([one, total - one])
    sizes = jnp.asarray(profile(count, total, limit, skew), jnp.int32)
    pairs = (count - 1) // 2
    donor, taker = sizes[1:1 + 2 * pairs:2], sizes[2:2 + 2 * pairs:2]
    margin = jnp.minimum(donor - 1, limit - taker)
    shifted = jax.random.randint(jax.random.fold_in(own_key, 1), (pairs,), 0, 1 << 20) % (margin + 1)
    sizes = sizes.at[1:1 + 2 * pairs:2].set(donor - shifted).at[2:2 + 2 * pairs:2].set(taker + shifted)
    return sizes[jax.random.permutation(jax.random.fold_in(own_key, 2), count)]


def bell_draw(own_key, shape, spread, most, cuts=(), kind=jnp.bfloat16):
    entries = jax.random.normal(own_key, shape, jnp.float32) * spread
    if len(cuts) > 0:
        entries = shard_levels(own_key, shape, cuts, -0.22, 0.18) * entries
    return jnp.clip(entries, min=-most, max=most).astype(kind)


def gaussian_with(own_key, dims, spread, bound, split, heavy, kind=jnp.bfloat16):
    values = spread * jax.random.normal(own_key, dims, jnp.float32)
    if split:
        values = values * shard_levels(own_key, dims, split, -0.22, 0.18)
    return jnp.clip(raised(values, jax.random.fold_in(own_key, 3), *heavy), -bound, bound).astype(kind)


def setup_inputs(seed: int = 0) -> dict:
    arg_keys = jax.random.split(jax.random.key(seed), 7)
    queries = draw_queries(jax.random.fold_in(arg_keys[6], 71), 0)
    keys = draw_keys(jax.random.fold_in(arg_keys[6], 71), 0)
    values = bell_draw(arg_keys[2], (TOKENS, HD), 1.0, 6.0, ((0, 32),))
    grad_out = gaussian_with(arg_keys[3], (TOKENS, D), 0.25, 2.0, ((0, 32),), (0, 1, 32, 2.75))
    out_weight = bell_draw(arg_keys[4], (D, HD), HD ** -0.5, 0.15625, ((0, 8), (1, 4)))
    clip_lengths = jax.vmap(lambda own: ragged(own, CLIPS, N_SEQ * TOK_DEV, 2 * TOK_DEV, 2))(jax.random.split(arg_keys[5], N_DP)).reshape((N_DP, CLIPS)).astype(jnp.int32)
    return {"queries": queries, "keys": keys, "values": values, "grad_out": grad_out, "out_weight": out_weight, "clip_lengths": clip_lengths}


def clip_index(lengths, count):
    ends = jnp.cumsum(lengths.astype(jnp.int32))
    positions = jnp.arange(count, dtype=jnp.int32)
    return jnp.sum((positions[:, None] >= ends[None, :]).astype(jnp.int32), axis=1)


def head_pass(head_queries, head_keys, head_values, head_grads, same_clip, scale):
    scores = jnp.dot(head_queries, head_keys.T, preferred_element_type=jnp.float32) * scale
    scores = jnp.where(same_clip, scores, -jnp.inf)
    top = jnp.max(scores, axis=1, keepdims=True)
    weights = jnp.exp(scores - top)
    probs = weights / jnp.sum(weights, axis=1, keepdims=True)
    probs_low = probs.astype(jnp.bfloat16)
    attention = jnp.dot(probs_low, head_values, preferred_element_type=jnp.float32).astype(jnp.bfloat16)
    attention = lax.optimization_barrier(attention)
    grad_values = jnp.dot(probs_low.T, head_grads, preferred_element_type=jnp.float32).astype(jnp.bfloat16)
    grad_probs = jnp.dot(head_grads, head_values.T, preferred_element_type=jnp.float32)
    delta = jnp.sum(head_grads.astype(jnp.float32) * attention.astype(jnp.float32), axis=1, keepdims=True)
    grad_scores = (probs * (grad_probs - delta) * scale).astype(jnp.bfloat16)
    grad_queries = jnp.dot(grad_scores, head_keys, preferred_element_type=jnp.float32).astype(jnp.bfloat16)
    grad_keys = jnp.dot(grad_scores.T, head_queries, preferred_element_type=jnp.float32).astype(jnp.bfloat16)
    return attention, grad_queries, grad_keys, grad_values


def reference(queries, keys, values, grad_out, out_weight, clip_lengths):
    group_tok = N_SEQ * TOK_DEV
    scale = HEAD_DIM ** -0.5
    grad_attention = jnp.dot(grad_out, out_weight, preferred_element_type=jnp.float32).astype(jnp.bfloat16)

    def split_heads(array):
        return array.reshape(N_DP, group_tok, HEADS, HEAD_DIM).transpose(0, 2, 1, 3)

    def one_group(pieces):
        group_queries, group_keys, group_values, group_grads, lengths = pieces
        clips = clip_index(lengths, group_tok)
        same_clip = clips[:, None] == clips[None, :]

        def one_head(head_pieces):
            return head_pass(head_pieces[0], head_pieces[1], head_pieces[2], head_pieces[3], same_clip, scale)

        return lax.map(one_head, (group_queries, group_keys, group_values, group_grads))

    results = lax.map(one_group, (split_heads(queries), split_heads(keys), split_heads(values), split_heads(grad_attention), clip_lengths))

    def join_heads(array):
        return array.transpose(0, 2, 1, 3).reshape(TOKENS, HD)

    attention = join_heads(results[0])
    grad_weight = jnp.dot(grad_out.T, attention, preferred_element_type=jnp.float32)
    return join_heads(results[1]), join_heads(results[2]), join_heads(results[3]), grad_weight
```

```python
import jax
import jax.numpy as jnp
from jax import lax
from jax.sharding import PartitionSpec as P

HEAD_DIM = 128


def clip_index(lengths, count):
    ends = jnp.cumsum(lengths)
    positions = jnp.arange(count, dtype=jnp.int32)
    return jnp.sum((positions[:, None] >= ends[None, :]).astype(jnp.int32), axis=1)


def body(queries, keys, values, grad_out, out_weight, clip_lengths):
    head_queries, head_keys, head_values = (
        lax.all_to_all(queries, "seq", split_axis=1, concat_axis=0, tiled=True),
        lax.all_to_all(keys, "seq", split_axis=1, concat_axis=0, tiled=True),
        lax.all_to_all(values, "seq", split_axis=1, concat_axis=0, tiled=True),
    )
    group_grads = lax.all_gather(grad_out, "seq", axis=0, tiled=True)
    weight_cols = lax.all_gather(out_weight, "dp", axis=0, tiled=True)
    head_grads = jnp.dot(
        group_grads, weight_cols, preferred_element_type=jnp.float32
    ).astype(jnp.bfloat16)
    group_len = head_queries.shape[0]
    local_heads = head_queries.shape[1] // HEAD_DIM
    scale = HEAD_DIM ** (-0.5)
    query_heads = head_queries.reshape(group_len, local_heads, HEAD_DIM)
    key_heads = head_keys.reshape(group_len, local_heads, HEAD_DIM)
    value_heads = head_values.reshape(group_len, local_heads, HEAD_DIM)
    grad_heads = head_grads.reshape(group_len, local_heads, HEAD_DIM)
    clips = clip_index(clip_lengths[0], group_len)
    block = min(512, group_len)
    blocks = group_len // block

    def step(carry, block_index):
        key_total, value_total = carry
        start = block_index * block
        query_block = lax.dynamic_slice_in_dim(query_heads, start, block, 0)
        grad_block = lax.dynamic_slice_in_dim(grad_heads, start, block, 0)
        clip_block = lax.dynamic_slice_in_dim(clips, start, block, 0)
        scores = (
            jnp.einsum("qhd,khd->hqk", query_block, key_heads, preferred_element_type=jnp.float32)
            * scale
        )
        same_clip = clip_block[:, None] == clips[None, :]
        scores = jnp.where(same_clip[None, :, :], scores, -jnp.inf)
        top = jnp.max(scores, axis=2, keepdims=True)
        weights = jnp.exp(scores - top)
        probs = weights / jnp.sum(weights, axis=2, keepdims=True)
        probs_low = probs.astype(jnp.bfloat16)
        attention = jnp.einsum(
            "hqk,khd->qhd", probs_low, value_heads, preferred_element_type=jnp.float32
        ).astype(jnp.bfloat16)
        attention = lax.optimization_barrier(attention)
        value_total = value_total + jnp.einsum(
            "hqk,qhd->khd", probs_low, grad_block, preferred_element_type=jnp.float32
        )
        grad_probs = jnp.einsum(
            "qhd,khd->hqk", grad_block, value_heads, preferred_element_type=jnp.float32
        )
        delta = jnp.sum(grad_block.astype(jnp.float32) * attention.astype(jnp.float32), axis=2).T
        grad_scores = (probs * (grad_probs - delta[:, :, None]) * scale).astype(jnp.bfloat16)
        grad_query_block = jnp.einsum(
            "hqk,khd->qhd", grad_scores, key_heads, preferred_element_type=jnp.float32
        ).astype(jnp.bfloat16)
        key_total = key_total + jnp.einsum(
            "hqk,qhd->khd", grad_scores, query_block, preferred_element_type=jnp.float32
        )
        return ((key_total, value_total), (attention, grad_query_block))

    empty = jnp.zeros((group_len, local_heads, HEAD_DIM), jnp.float32)
    totals, outputs = lax.scan(step, (empty, empty), jnp.arange(blocks, dtype=jnp.int32))
    width = local_heads * HEAD_DIM
    attention_flat = outputs[0].reshape(group_len, width)
    grad_query_heads = outputs[1].reshape(group_len, width)
    grad_key_heads = totals[0].reshape(group_len, width).astype(jnp.bfloat16)
    grad_value_heads = totals[1].reshape(group_len, width).astype(jnp.bfloat16)
    partial = lax.dot_general(
        group_grads,
        attention_flat,
        (((0,), (0,)), ((), ())),
        preferred_element_type=jnp.float32,
    ).astype(jnp.bfloat16)
    out_rows = out_weight.shape[0]
    pieces = lax.all_to_all(partial, "dp", split_axis=0, concat_axis=0, tiled=True)
    grad_weight = jnp.sum(
        pieces.reshape(-1, out_rows, width).astype(jnp.float32), axis=0
    )
    grad_queries, grad_keys, grad_values = (
        lax.all_to_all(grad_query_heads, "seq", split_axis=0, concat_axis=1, tiled=True),
        lax.all_to_all(grad_key_heads, "seq", split_axis=0, concat_axis=1, tiled=True),
        lax.all_to_all(grad_value_heads, "seq", split_axis=0, concat_axis=1, tiled=True),
    )
    return (grad_queries, grad_keys, grad_values, grad_weight)


def solution(mesh):
    placed = (
        P(("dp", "seq"), None),
        P(("dp", "seq"), None),
        P(("dp", "seq"), None),
        P(("dp", "seq"), None),
        P("dp", "seq"),
        P("dp", None),
    )
    return jax.shard_map(
        body,
        mesh=mesh,
        in_specs=placed,
        out_specs=(
            P(("dp", "seq"), None),
            P(("dp", "seq"), None),
            P(("dp", "seq"), None),
            P("dp", "seq"),
        ),
        check_vma=False,
    )
```

```python
import functools

import jax
import jax.numpy as jnp
from jax import lax
from jax.experimental import pallas as pl
from jax.experimental.pallas import tpu as pltpu
from jax.sharding import PartitionSpec as P

HEAD_DIM = 128
MESH = pl.DeviceIdType.MESH


def mul(a, b, da, db):
    return lax.dot_general(a, b, (((da,), (db,)), ((), ())), preferred_element_type=jnp.float32)


def kernel(n_dp, n_seq, q, k, v, go, w, cl, gq, gk, gv, gw,
           hq, hk, hv, gg, wc, oq, ok, ov, gk_acc, gv_acc, gw_acc, part, recv, att, ga,
           s_in, r_in, s_w, r_w, s_left, s_right, r_g, s_out, r_out, s_p, r_p, s_own):
    dp, me = lax.axis_index("dp"), lax.axis_index("seq")
    tok = q.shape[0]
    group = tok * n_seq
    width = hq.shape[1]
    heads = width // HEAD_DIM
    wrows = w.shape[0]
    d_out = go.shape[1]
    scale = HEAD_DIM ** (-0.5)

    def toks(i):
        return pl.ds(pl.multiple_of(i * tok, tok), tok)

    def cols(i):
        return pl.ds(pl.multiple_of(i * width, width), width)

    def feats(i):
        return pl.ds(pl.multiple_of(i * wrows, wrows), wrows)

    def remote(src, dst, ssem, rsem, **device):
        return pltpu.make_async_remote_copy(
            src_ref=src, dst_ref=dst, send_sem=ssem, recv_sem=rsem,
            device_id=device, device_id_type=MESH)

    barrier = pltpu.get_barrier_semaphore()
    for d in range(1, n_seq):
        pl.semaphore_signal(barrier, inc=1, device_id={"seq": lax.rem(me + d, n_seq)}, device_id_type=MESH)

    @pl.loop(1, n_dp)
    def _(d):
        pl.semaphore_signal(barrier, inc=1, device_id={"dp": lax.rem(dp + d, n_dp)}, device_id_type=MESH)

    own = [
        pltpu.make_async_copy(q.at[:, cols(me)], hq.at[toks(me), :], s_own.at[0]),
        pltpu.make_async_copy(k.at[:, cols(me)], hk.at[toks(me), :], s_own.at[1]),
        pltpu.make_async_copy(v.at[:, cols(me)], hv.at[toks(me), :], s_own.at[2]),
        pltpu.make_async_copy(go, gg.at[me], s_own.at[3]),
        pltpu.make_async_copy(w, wc.at[feats(dp), :], s_own.at[4]),
    ]
    for c in own:
        c.start()
    pl.semaphore_wait(barrier, n_seq - 1 + n_dp - 1)

    def exchange(i, src, dst, frm, to):
        return remote(src.at[:, cols(to)], dst.at[toks(frm), :], s_in.at[i, to], r_in.at[i, frm], seq=to)

    def to_right(b):
        src = gg.at[b]
        return remote(src, gg.at[b], s_right.at[b], r_g.at[b], seq=lax.rem(me + 1, n_seq))

    def to_left(b):
        return remote(gg.at[b], gg.at[b], s_left.at[b], r_g.at[b], seq=lax.rem(me + n_seq - 1, n_seq))

    def weight(frm, to):
        return remote(w, wc.at[feats(frm), :], s_w.at[to], r_w.at[frm], dp=to)

    pairs = ((q, hq), (k, hk), (v, hv))
    own[3].wait()

    @pl.when(me < n_seq - 1)
    def _():
        to_right(me).start()

    @pl.when(me > 0)
    def _():
        to_left(me).start()

    for d in range(1, n_seq):
        to = lax.rem(me + d, n_seq)
        for i, (src, dst) in enumerate(pairs):
            exchange(i, src, dst, me, to).start()

    @pl.loop(1, n_dp)
    def _(d):
        weight(dp, lax.rem(dp + d, n_dp)).start()

    gk_acc[...] = jnp.zeros_like(gk_acc)
    gv_acc[...] = jnp.zeros_like(gv_acc)
    gw_acc[...] = jnp.zeros_like(gw_acc)
    for i in (0, 1, 2, 4):
        own[i].wait()

    @pl.loop(1, n_dp)
    def _(d):
        frm = lax.rem(dp + d, n_dp)
        weight(frm, frm).wait_recv()

    for d in range(1, n_seq):
        frm = lax.rem(me + d, n_seq)
        for i, (src, dst) in enumerate(pairs):
            exchange(i, src, dst, frm, frm).wait_recv()

    def clip_of(positions):
        index, end = jnp.zeros_like(positions), 0
        for c in range(cl.shape[1]):
            end = end + cl[0, c]
            index = index + jnp.where(positions >= end, 1, 0)
        return index

    def returned(i, src, dst, frm, to):
        return remote(src.at[toks(to), :], dst.at[:, cols(frm)], s_out.at[i, to], r_out.at[i, frm], seq=to)

    def work(b):
        ga[...] = mul(gg[b], wc[...], 1, 0).astype(jnp.bfloat16)
        same = (clip_of(lax.broadcasted_iota(jnp.int32, (tok, 1), 0) + b * tok)
                == clip_of(lax.broadcasted_iota(jnp.int32, (1, group), 1)))
        for h in range(heads):
            c = slice(h * HEAD_DIM, (h + 1) * HEAD_DIM)
            qh, gh = hq[toks(b), c], ga[:, c]
            kh, vh = hk[:, c], hv[:, c]
            scores = jnp.where(same, mul(qh, kh, 1, 1) * scale, -jnp.inf)
            top = jnp.max(scores, axis=1, keepdims=True)
            weights = jnp.exp(scores - top)
            probs = weights * (1.0 / jnp.sum(weights, axis=1, keepdims=True))
            low = probs.astype(jnp.bfloat16)
            ah = mul(low, vh, 1, 0).astype(jnp.bfloat16)
            att[:, c] = ah
            gv_acc[:, c] += mul(low, gh, 0, 0)
            delta = jnp.sum(gh.astype(jnp.float32) * ah.astype(jnp.float32), axis=1, keepdims=True)
            gs = (probs * (mul(gh, vh, 1, 1) - delta) * scale).astype(jnp.bfloat16)
            oq[toks(b), c] = mul(gs, kh, 1, 0).astype(jnp.bfloat16)
            gk_acc[:, c] += mul(gs, qh, 0, 0)
        step = min(512, d_out)
        for f in range(0, d_out, step):
            gw_acc[f:f + step, :] += mul(gg[b, :, f:f + step], att[...], 0, 0)

    @pl.loop(0, 2 * n_seq - 1)
    def _(j):
        s, side = (j + 1) // 2, j % 2
        b = jnp.where(side == 1, me - s, me + s)

        @pl.when((b >= 0) & (b < n_seq))
        def _():
            @pl.when(b < me)
            def _():
                to_right(b).wait_recv()

                @pl.when(me < n_seq - 1)
                def _():
                    to_right(b).start()

            @pl.when(b > me)
            def _():
                to_left(b).wait_recv()

                @pl.when(me > 0)
                def _():
                    to_left(b).start()

            work(b)

            @pl.when(b != me)
            def _():
                returned(0, oq, gq, me, b).start()

    ok[...] = gk_acc[...].astype(jnp.bfloat16)
    ov[...] = gv_acc[...].astype(jnp.bfloat16)
    for d in range(1, n_seq):
        to = lax.rem(me + d, n_seq)
        returned(1, ok, gk, me, to).start()
        returned(2, ov, gv, me, to).start()
    part[...] = gw_acc[...].astype(jnp.bfloat16)

    def partial(frm, to):
        return remote(part.at[feats(to), :], recv.at[frm], s_p.at[to], r_p.at[frm], dp=to)

    @pl.loop(1, n_dp)
    def _(d):
        partial(dp, lax.rem(dp + d, n_dp)).start()

    kept = [
        pltpu.make_async_copy(oq.at[toks(me), :], gq.at[:, cols(me)], s_own.at[0]),
        pltpu.make_async_copy(ok.at[toks(me), :], gk.at[:, cols(me)], s_own.at[1]),
        pltpu.make_async_copy(ov.at[toks(me), :], gv.at[:, cols(me)], s_own.at[2]),
    ]
    for c in kept:
        c.start()
    gw[...] = gw_acc[feats(dp), :]

    @pl.loop(1, n_dp)
    def _(d):
        frm = lax.rem(dp + n_dp - d, n_dp)
        partial(frm, frm).wait_recv()
        gw[...] += recv[frm].astype(jnp.float32)

    for c in kept:
        c.wait()
    for d in range(1, n_seq):
        frm = lax.rem(me + d, n_seq)
        for i, (src, dst) in enumerate(((oq, gq), (ok, gk), (ov, gv))):
            returned(i, src, dst, frm, frm).wait_recv()
            returned(i, src, dst, me, frm).wait_send()
        for i, (src, dst) in enumerate(pairs):
            exchange(i, src, dst, me, frm).wait_send()

    @pl.loop(1, n_dp)
    def _(d):
        to = lax.rem(dp + d, n_dp)
        weight(dp, to).wait_send()
        partial(dp, to).wait_send()

    @pl.loop(0, n_seq)
    def _(b):
        @pl.when((b <= me) & (me < n_seq - 1))
        def _():
            to_right(b).wait_send()

        @pl.when((b >= me) & (me > 0))
        def _():
            to_left(b).wait_send()


def body(n_dp, n_seq, queries, keys, values, grad_out, out_weight, clip_lengths):
    tok, all_width = queries.shape
    d_out = grad_out.shape[1]
    wrows, width = out_weight.shape
    group = tok * n_seq
    bf, f32 = jnp.bfloat16, jnp.float32
    vmem = pl.BlockSpec(memory_space=pltpu.VMEM)
    dma = pltpu.SemaphoreType.DMA
    return tuple(pl.pallas_call(
        functools.partial(kernel, n_dp, n_seq),
        out_shape=(jax.ShapeDtypeStruct((tok, all_width), bf),) * 3
        + (jax.ShapeDtypeStruct((wrows, width), f32),),
        in_specs=[vmem] * 5 + [pl.BlockSpec(memory_space=pltpu.SMEM)],
        out_specs=(vmem,) * 4,
        scratch_shapes=[pltpu.VMEM((group, width), bf)] * 3
        + [pltpu.VMEM((n_seq, tok, d_out), bf), pltpu.VMEM((d_out, width), bf)]
        + [pltpu.VMEM((group, width), bf)] * 3
        + [pltpu.VMEM((group, width), f32)] * 2
        + [pltpu.VMEM((d_out, width), f32), pltpu.VMEM((d_out, width), bf),
           pltpu.VMEM((n_dp, wrows, width), bf),
           pltpu.VMEM((tok, width), bf), pltpu.VMEM((tok, width), bf)]
        + [dma((3, n_seq)), dma((3, n_seq)), dma((n_dp,)), dma((n_dp,)),
           dma((n_seq,)), dma((n_seq,)), dma((n_seq,)),
           dma((3, n_seq)), dma((3, n_seq)), dma((n_dp,)), dma((n_dp,)), dma((5,))],
        compiler_params=pltpu.CompilerParams(
            collective_id=0, has_side_effects=True, vmem_limit_bytes=56 * 1024 * 1024),
        cost_estimate=pl.CostEstimate(
            flops=2 * group * width * (2 * d_out + 6 * group),
            bytes_accessed=16 * tok * all_width, transcendentals=group * group * width // HEAD_DIM),
    )(queries, keys, values, grad_out, out_weight, clip_lengths))


def solution(mesh):
    placed = (
        P(("dp", "seq"), None),
        P(("dp", "seq"), None),
        P(("dp", "seq"), None),
        P(("dp", "seq"), None),
        P("dp", "seq"),
        P("dp", None),
    )
    return jax.shard_map(
        functools.partial(body, mesh.shape["dp"], mesh.shape["seq"]),
        mesh=mesh,
        in_specs=placed,
        out_specs=(
            P(("dp", "seq"), None),
            P(("dp", "seq"), None),
            P(("dp", "seq"), None),
            P("dp", "seq"),
        ),
        check_vma=False,
    )
```

```python
import functools

import jax
import jax.numpy as jnp
from jax import lax
from jax.experimental import pallas as pl
from jax.experimental.pallas import tpu as pltpu
from jax.sharding import PartitionSpec as P

HEAD_DIM = 128
MESH = pl.DeviceIdType.MESH


def mul(a, b, da, db):
    return lax.dot_general(a, b, (((da,), (db,)), ((), ())), preferred_element_type=jnp.float32)


def kernel(n_dp, n_seq, q, k, v, go, w, cl, gq, gk, gv, gw,
           hq, hk, hv, gg, wc, oq, ok, ov, gk_acc, gv_acc, gw_acc, part, recv, att, ga,
           s_in, r_in, s_w, r_w, s_left, s_right, r_g, s_out, r_out, s_p, r_p, s_own):
    dp, me = lax.axis_index("dp"), lax.axis_index("seq")
    tok = q.shape[0]
    group = tok * n_seq
    width = hq.shape[1]
    heads = width // HEAD_DIM
    wrows = w.shape[0]
    d_out = go.shape[1]
    scale = HEAD_DIM ** (-0.5)

    def toks(i):
        return pl.ds(pl.multiple_of(i * tok, tok), tok)

    def cols(i):
        return pl.ds(pl.multiple_of(i * width, width), width)

    def feats(i):
        return pl.ds(pl.multiple_of(i * wrows, wrows), wrows)

    def remote(src, dst, ssem, rsem, **device):
        return pltpu.make_async_remote_copy(
            src_ref=src, dst_ref=dst, send_sem=ssem, recv_sem=rsem,
            device_id=device, device_id_type=MESH)

    barrier = pltpu.get_barrier_semaphore()
    for d in range(1, n_seq):
        pl.semaphore_signal(barrier, inc=1, device_id={"seq": lax.rem(me + d, n_seq)}, device_id_type=MESH)

    @pl.loop(1, n_dp)
    def _(d):
        pl.semaphore_signal(barrier, inc=1, device_id={"dp": lax.rem(dp + d, n_dp)}, device_id_type=MESH)

    own = [
        pltpu.make_async_copy(q.at[:, cols(me)], hq.at[toks(me), :], s_own.at[0]),
        pltpu.make_async_copy(k.at[:, cols(me)], hk.at[toks(me), :], s_own.at[1]),
        pltpu.make_async_copy(v.at[:, cols(me)], hv.at[toks(me), :], s_own.at[2]),
        pltpu.make_async_copy(go, gg.at[me], s_own.at[3]),
        pltpu.make_async_copy(w, wc.at[feats(dp), :], s_own.at[4]),
    ]
    for c in own:
        c.start()
    pl.semaphore_wait(barrier, n_seq - 1 + n_dp - 1)

    def exchange(i, src, dst, frm, to):
        return remote(src.at[:, cols(to)], dst.at[toks(frm), :], s_in.at[i, to], r_in.at[i, frm], seq=to)

    def to_right(b):
        src = gg.at[b]
        return remote(src, gg.at[b], s_right.at[b], r_g.at[b], seq=lax.rem(me + 1, n_seq))

    def to_left(b):
        return remote(gg.at[b], gg.at[b], s_left.at[b], r_g.at[b], seq=lax.rem(me + n_seq - 1, n_seq))

    def weight(frm, to):
        return remote(w, wc.at[feats(frm), :], s_w.at[to], r_w.at[frm], dp=to)

    pairs = ((q, hq), (k, hk), (v, hv))
    own[3].wait()

    @pl.when(me < n_seq - 1)
    def _():
        to_right(me).start()

    @pl.when(me > 0)
    def _():
        to_left(me).start()

    for d in range(1, n_seq):
        to = lax.rem(me + d, n_seq)
        for i, (src, dst) in enumerate(pairs):
            exchange(i, src, dst, me, to).start()

    @pl.loop(1, n_dp)
    def _(d):
        weight(dp, lax.rem(dp + d, n_dp)).start()

    def turn(j):
        s = (j + 1) // 2
        return jnp.where(j % 2 == 1, me - s, me + s)

    def relay(j):
        b = turn(j)

        @pl.when((b >= 0) & (b < me) & (me < n_seq - 1))
        def _():
            to_right(b).wait_recv()
            to_right(b).start()

        @pl.when((b > me) & (b < n_seq) & (me > 0))
        def _():
            to_left(b).wait_recv()
            to_left(b).start()

    gk_acc[...] = jnp.zeros_like(gk_acc)
    gv_acc[...] = jnp.zeros_like(gv_acc)
    gw_acc[...] = jnp.zeros_like(gw_acc)
    for i in (0, 1, 2, 4):
        own[i].wait()

    relay(1)
    relay(2)

    @pl.loop(1, n_dp)
    def _(d):
        frm = lax.rem(dp + d, n_dp)
        weight(frm, frm).wait_recv()

    for d in range(1, n_seq):
        frm = lax.rem(me + d, n_seq)
        for i, (src, dst) in enumerate(pairs):
            exchange(i, src, dst, frm, frm).wait_recv()

    def clip_of(positions):
        index, end = jnp.zeros_like(positions), 0
        for c in range(cl.shape[1]):
            end = end + cl[0, c]
            index = index + jnp.where(positions >= end, 1, 0)
        return index

    def returned(i, src, dst, frm, to):
        return remote(src.at[toks(to), :], dst.at[:, cols(frm)], s_out.at[i, to], r_out.at[i, frm], seq=to)

    def work(b):
        ga[...] = mul(gg[b], wc[...], 1, 0).astype(jnp.bfloat16)
        same = (clip_of(lax.broadcasted_iota(jnp.int32, (tok, 1), 0) + b * tok)
                == clip_of(lax.broadcasted_iota(jnp.int32, (1, group), 1)))
        for h in range(heads):
            c = slice(h * HEAD_DIM, (h + 1) * HEAD_DIM)
            qh, gh = hq[toks(b), c], ga[:, c]
            kh, vh = hk[:, c], hv[:, c]
            scores = jnp.where(same, mul(qh, kh, 1, 1) * scale, -jnp.inf)
            top = jnp.max(scores, axis=1, keepdims=True)
            weights = jnp.exp(scores - top)
            probs = weights * (1.0 / jnp.sum(weights, axis=1, keepdims=True))
            low = probs.astype(jnp.bfloat16)
            ah = mul(low, vh, 1, 0).astype(jnp.bfloat16)
            att[:, c] = ah
            gv_acc[:, c] += mul(low, gh, 0, 0)
            delta = jnp.sum(gh.astype(jnp.float32) * ah.astype(jnp.float32), axis=1, keepdims=True)
            gs = (probs * (mul(gh, vh, 1, 1) - delta) * scale).astype(jnp.bfloat16)
            oq[toks(b), c] = mul(gs, kh, 1, 0).astype(jnp.bfloat16)
            gk_acc[:, c] += mul(gs, qh, 0, 0)
        step = min(512, d_out)
        for f in range(0, d_out, step):
            gw_acc[f:f + step, :] += mul(gg[b, :, f:f + step], att[...], 0, 0)

    @pl.loop(0, 2 * n_seq - 1)
    def _(j):
        @pl.when((j % 2 == 0) & (j >= 2))
        def _():
            relay(j + 1)
            relay(j + 2)

        b = turn(j)

        @pl.when((b >= 0) & (b < n_seq))
        def _():
            @pl.when((b < me) & (me == n_seq - 1))
            def _():
                to_right(b).wait_recv()

            @pl.when((b > me) & (me == 0))
            def _():
                to_left(b).wait_recv()

            work(b)

            @pl.when(b != me)
            def _():
                returned(0, oq, gq, me, b).start()

    ok[...] = gk_acc[...].astype(jnp.bfloat16)
    ov[...] = gv_acc[...].astype(jnp.bfloat16)
    for d in range(1, n_seq):
        to = lax.rem(me + d, n_seq)
        returned(1, ok, gk, me, to).start()
        returned(2, ov, gv, me, to).start()
    part[...] = gw_acc[...].astype(jnp.bfloat16)

    def partial(frm, to):
        return remote(part.at[feats(to), :], recv.at[frm], s_p.at[to], r_p.at[frm], dp=to)

    @pl.loop(1, n_dp)
    def _(d):
        partial(dp, lax.rem(dp + d, n_dp)).start()

    kept = [
        pltpu.make_async_copy(oq.at[toks(me), :], gq.at[:, cols(me)], s_own.at[0]),
        pltpu.make_async_copy(ok.at[toks(me), :], gk.at[:, cols(me)], s_own.at[1]),
        pltpu.make_async_copy(ov.at[toks(me), :], gv.at[:, cols(me)], s_own.at[2]),
    ]
    for c in kept:
        c.start()
    gw[...] = gw_acc[feats(dp), :]

    @pl.loop(1, n_dp)
    def _(d):
        frm = lax.rem(dp + n_dp - d, n_dp)
        partial(frm, frm).wait_recv()
        gw[...] += recv[frm].astype(jnp.float32)

    for c in kept:
        c.wait()
    for d in range(1, n_seq):
        frm = lax.rem(me + d, n_seq)
        for i, (src, dst) in enumerate(((oq, gq), (ok, gk), (ov, gv))):
            returned(i, src, dst, frm, frm).wait_recv()
            returned(i, src, dst, me, frm).wait_send()
        for i, (src, dst) in enumerate(pairs):
            exchange(i, src, dst, me, frm).wait_send()

    @pl.loop(1, n_dp)
    def _(d):
        to = lax.rem(dp + d, n_dp)
        weight(dp, to).wait_send()
        partial(dp, to).wait_send()

    @pl.loop(0, n_seq)
    def _(b):
        @pl.when((b <= me) & (me < n_seq - 1))
        def _():
            to_right(b).wait_send()

        @pl.when((b >= me) & (me > 0))
        def _():
            to_left(b).wait_send()


def body(n_dp, n_seq, queries, keys, values, grad_out, out_weight, clip_lengths):
    tok, all_width = queries.shape
    d_out = grad_out.shape[1]
    wrows, width = out_weight.shape
    group = tok * n_seq
    bf, f32 = jnp.bfloat16, jnp.float32
    vmem = pl.BlockSpec(memory_space=pltpu.VMEM)
    dma = pltpu.SemaphoreType.DMA
    return tuple(pl.pallas_call(
        functools.partial(kernel, n_dp, n_seq),
        out_shape=(jax.ShapeDtypeStruct((tok, all_width), bf),) * 3
        + (jax.ShapeDtypeStruct((wrows, width), f32),),
        in_specs=[vmem] * 5 + [pl.BlockSpec(memory_space=pltpu.SMEM)],
        out_specs=(vmem,) * 4,
        scratch_shapes=[pltpu.VMEM((group, width), bf)] * 3
        + [pltpu.VMEM((n_seq, tok, d_out), bf), pltpu.VMEM((d_out, width), bf)]
        + [pltpu.VMEM((group, width), bf)] * 3
        + [pltpu.VMEM((group, width), f32)] * 2
        + [pltpu.VMEM((d_out, width), f32), pltpu.VMEM((d_out, width), bf),
           pltpu.VMEM((n_dp, wrows, width), bf),
           pltpu.VMEM((tok, width), bf), pltpu.VMEM((tok, width), bf)]
        + [dma((3, n_seq)), dma((3, n_seq)), dma((n_dp,)), dma((n_dp,)),
           dma((n_seq,)), dma((n_seq,)), dma((n_seq,)),
           dma((3, n_seq)), dma((3, n_seq)), dma((n_dp,)), dma((n_dp,)), dma((5,))],
        compiler_params=pltpu.CompilerParams(
            collective_id=0, has_side_effects=True, vmem_limit_bytes=56 * 1024 * 1024),
        cost_estimate=pl.CostEstimate(
            flops=2 * group * width * (2 * d_out + 6 * group),
            bytes_accessed=16 * tok * all_width, transcendentals=group * group * width // HEAD_DIM),
    )(queries, keys, values, grad_out, out_weight, clip_lengths))


def solution(mesh):
    placed = (
        P(("dp", "seq"), None),
        P(("dp", "seq"), None),
        P(("dp", "seq"), None),
        P(("dp", "seq"), None),
        P("dp", "seq"),
        P("dp", None),
    )
    return jax.shard_map(
        functools.partial(body, mesh.shape["dp"], mesh.shape["seq"]),
        mesh=mesh,
        in_specs=placed,
        out_specs=(
            P(("dp", "seq"), None),
            P(("dp", "seq"), None),
            P(("dp", "seq"), None),
            P("dp", "seq"),
        ),
        check_vma=False,
    )
```

```python
import functools

import jax
import jax.numpy as jnp
from jax import lax
from jax.experimental import pallas as pl
from jax.experimental.pallas import tpu as pltpu
from jax.sharding import PartitionSpec as P

HEAD_DIM = 128
MESH = pl.DeviceIdType.MESH


def mul(a, b, da, db):
    return lax.dot_general(a, b, (((da,), (db,)), ((), ())), preferred_element_type=jnp.float32)


def kernel(n_dp, n_seq, q, k, v, go, w, cl, gq, gk, gv, gw,
           hq, hk, hv, gg, wc, oq, ok, ov, gk_acc, gv_acc, gw_acc, part, recv, att, ga,
           s_in, r_in, s_w, r_w, s_left, s_right, r_g, s_out, r_out, s_p, r_p, s_own):
    dp, me = lax.axis_index("dp"), lax.axis_index("seq")
    tok = q.shape[0]
    group = tok * n_seq
    width = hq.shape[1]
    heads = width // HEAD_DIM
    wrows = w.shape[0]
    d_out = go.shape[1]
    scale = HEAD_DIM ** (-0.5)

    def toks(i):
        return pl.ds(pl.multiple_of(i * tok, tok), tok)

    def cols(i):
        return pl.ds(pl.multiple_of(i * width, width), width)

    def feats(i):
        return pl.ds(pl.multiple_of(i * wrows, wrows), wrows)

    def remote(src, dst, ssem, rsem, **device):
        return pltpu.make_async_remote_copy(
            src_ref=src, dst_ref=dst, send_sem=ssem, recv_sem=rsem,
            device_id=device, device_id_type=MESH)

    barrier = pltpu.get_barrier_semaphore()
    for d in range(1, n_seq):
        pl.semaphore_signal(barrier, inc=1, device_id={"seq": lax.rem(me + d, n_seq)}, device_id_type=MESH)

    @pl.loop(1, n_dp)
    def _(d):
        pl.semaphore_signal(barrier, inc=1, device_id={"dp": lax.rem(dp + d, n_dp)}, device_id_type=MESH)

    own = [
        pltpu.make_async_copy(q.at[:, cols(me)], hq.at[toks(me), :], s_own.at[0]),
        pltpu.make_async_copy(k.at[:, cols(me)], hk.at[toks(me), :], s_own.at[1]),
        pltpu.make_async_copy(v.at[:, cols(me)], hv.at[toks(me), :], s_own.at[2]),
        pltpu.make_async_copy(go, gg.at[me], s_own.at[3]),
        pltpu.make_async_copy(w, wc.at[feats(dp), :], s_own.at[4]),
    ]
    for c in own:
        c.start()
    pl.semaphore_wait(barrier, n_seq - 1 + n_dp - 1)

    def exchange(i, src, dst, frm, to):
        return remote(src.at[:, cols(to)], dst.at[toks(frm), :], s_in.at[i, to], r_in.at[i, frm], seq=to)

    def to_right(b):
        src = gg.at[b]
        return remote(src, gg.at[b], s_right.at[b], r_g.at[b], seq=lax.rem(me + 1, n_seq))

    def to_left(b):
        return remote(gg.at[b], gg.at[b], s_left.at[b], r_g.at[b], seq=lax.rem(me + n_seq - 1, n_seq))

    def weight(frm, to):
        return remote(w, wc.at[feats(frm), :], s_w.at[to], r_w.at[frm], dp=to)

    pairs = ((q, hq), (k, hk), (v, hv))
    own[3].wait()

    @pl.when(me < n_seq - 1)
    def _():
        to_right(me).start()

    @pl.when(me > 0)
    def _():
        to_left(me).start()

    for d in range(1, n_seq):
        to = lax.rem(me + d, n_seq)
        for i, (src, dst) in enumerate(pairs):
            exchange(i, src, dst, me, to).start()

    @pl.loop(1, n_dp)
    def _(d):
        weight(dp, lax.rem(dp + d, n_dp)).start()

    def turn(j):
        s = (j + 1) // 2
        return jnp.where(j % 2 == 1, me - s, me + s)

    def relay(j):
        b = turn(j)

        @pl.when((b >= 0) & (b < me) & (me < n_seq - 1))
        def _():
            to_right(b).wait_recv()
            to_right(b).start()

        @pl.when((b > me) & (b < n_seq) & (me > 0))
        def _():
            to_left(b).wait_recv()
            to_left(b).start()

    gk_acc[...] = jnp.zeros_like(gk_acc)
    gv_acc[...] = jnp.zeros_like(gv_acc)
    for i in (0, 1, 2, 4):
        own[i].wait()

    relay(1)
    relay(2)

    @pl.loop(1, n_dp)
    def _(d):
        frm = lax.rem(dp + d, n_dp)
        weight(frm, frm).wait_recv()

    for d in range(1, n_seq):
        frm = lax.rem(me + d, n_seq)
        for i, (src, dst) in enumerate(pairs):
            exchange(i, src, dst, frm, frm).wait_recv()

    def clip_of(positions):
        index, end = jnp.zeros_like(positions), 0
        for c in range(cl.shape[1]):
            end = end + cl[0, c]
            index = index + jnp.where(positions >= end, 1, 0)
        return index

    def returned(i, src, dst, frm, to):
        return remote(src.at[toks(to), :], dst.at[:, cols(frm)], s_out.at[i, to], r_out.at[i, frm], seq=to)

    def work(b):
        ga[...] = mul(gg[b], wc[...], 1, 0).astype(jnp.bfloat16)
        same = (clip_of(lax.broadcasted_iota(jnp.int32, (tok, 1), 0) + b * tok)
                == clip_of(lax.broadcasted_iota(jnp.int32, (1, group), 1)))
        for h in range(heads):
            c = slice(h * HEAD_DIM, (h + 1) * HEAD_DIM)
            qh, gh = hq[toks(b), c], ga[:, c]
            kh, vh = hk[:, c], hv[:, c]
            scores = jnp.where(same, mul(qh, kh, 1, 1) * scale, -jnp.inf)
            top = jnp.max(scores, axis=1, keepdims=True)
            weights = jnp.exp(scores - top)
            probs = weights * (1.0 / jnp.sum(weights, axis=1, keepdims=True))
            low = probs.astype(jnp.bfloat16)
            ah = mul(low, vh, 1, 0).astype(jnp.bfloat16)
            att[toks(b), c] = ah
            gv_acc[:, c] += mul(low, gh, 0, 0)
            delta = jnp.sum(gh.astype(jnp.float32) * ah.astype(jnp.float32), axis=1, keepdims=True)
            gs = (probs * (mul(gh, vh, 1, 1) - delta) * scale).astype(jnp.bfloat16)
            oq[toks(b), c] = mul(gs, kh, 1, 0).astype(jnp.bfloat16)
            gk_acc[:, c] += mul(gs, qh, 0, 0)

    @pl.loop(0, 2 * n_seq - 1)
    def _(j):
        @pl.when((j % 2 == 0) & (j >= 2))
        def _():
            relay(j + 1)
            relay(j + 2)

        b = turn(j)

        @pl.when((b >= 0) & (b < n_seq))
        def _():
            @pl.when((b < me) & (me == n_seq - 1))
            def _():
                to_right(b).wait_recv()

            @pl.when((b > me) & (me == 0))
            def _():
                to_left(b).wait_recv()

            work(b)

            @pl.when(b != me)
            def _():
                returned(0, oq, gq, me, b).start()

    ok[...] = gk_acc[...].astype(jnp.bfloat16)
    ov[...] = gv_acc[...].astype(jnp.bfloat16)
    for d in range(1, n_seq):
        to = lax.rem(me + d, n_seq)
        returned(1, ok, gk, me, to).start()
        returned(2, ov, gv, me, to).start()
    step = min(512, d_out)
    for f in range(0, d_out, step):
        total = mul(gg[:, :, f:f + step].reshape(group, step), att[...], 0, 0)
        gw_acc[f:f + step, :] = total
        part[f:f + step, :] = total.astype(jnp.bfloat16)

    def partial(frm, to):
        return remote(part.at[feats(to), :], recv.at[frm], s_p.at[to], r_p.at[frm], dp=to)

    @pl.loop(1, n_dp)
    def _(d):
        partial(dp, lax.rem(dp + d, n_dp)).start()

    kept = [
        pltpu.make_async_copy(oq.at[toks(me), :], gq.at[:, cols(me)], s_own.at[0]),
        pltpu.make_async_copy(ok.at[toks(me), :], gk.at[:, cols(me)], s_own.at[1]),
        pltpu.make_async_copy(ov.at[toks(me), :], gv.at[:, cols(me)], s_own.at[2]),
    ]
    for c in kept:
        c.start()
    gw[...] = gw_acc[feats(dp), :]

    @pl.loop(1, n_dp)
    def _(d):
        frm = lax.rem(dp + n_dp - d, n_dp)
        partial(frm, frm).wait_recv()
        gw[...] += recv[frm].astype(jnp.float32)

    for c in kept:
        c.wait()
    for d in range(1, n_seq):
        frm = lax.rem(me + d, n_seq)
        for i, (src, dst) in enumerate(((oq, gq), (ok, gk), (ov, gv))):
            returned(i, src, dst, frm, frm).wait_recv()
            returned(i, src, dst, me, frm).wait_send()
        for i, (src, dst) in enumerate(pairs):
            exchange(i, src, dst, me, frm).wait_send()

    @pl.loop(1, n_dp)
    def _(d):
        to = lax.rem(dp + d, n_dp)
        weight(dp, to).wait_send()
        partial(dp, to).wait_send()

    @pl.loop(0, n_seq)
    def _(b):
        @pl.when((b <= me) & (me < n_seq - 1))
        def _():
            to_right(b).wait_send()

        @pl.when((b >= me) & (me > 0))
        def _():
            to_left(b).wait_send()


def body(n_dp, n_seq, queries, keys, values, grad_out, out_weight, clip_lengths):
    tok, all_width = queries.shape
    d_out = grad_out.shape[1]
    wrows, width = out_weight.shape
    group = tok * n_seq
    bf, f32 = jnp.bfloat16, jnp.float32
    vmem = pl.BlockSpec(memory_space=pltpu.VMEM)
    dma = pltpu.SemaphoreType.DMA
    return tuple(pl.pallas_call(
        functools.partial(kernel, n_dp, n_seq),
        out_shape=(jax.ShapeDtypeStruct((tok, all_width), bf),) * 3
        + (jax.ShapeDtypeStruct((wrows, width), f32),),
        in_specs=[vmem] * 5 + [pl.BlockSpec(memory_space=pltpu.SMEM)],
        out_specs=(vmem,) * 4,
        scratch_shapes=[pltpu.VMEM((group, width), bf)] * 3
        + [pltpu.VMEM((n_seq, tok, d_out), bf), pltpu.VMEM((d_out, width), bf)]
        + [pltpu.VMEM((group, width), bf)] * 3
        + [pltpu.VMEM((group, width), f32)] * 2
        + [pltpu.VMEM((d_out, width), f32), pltpu.VMEM((d_out, width), bf),
           pltpu.VMEM((n_dp, wrows, width), bf),
           pltpu.VMEM((group, width), bf), pltpu.VMEM((tok, width), bf)]
        + [dma((3, n_seq)), dma((3, n_seq)), dma((n_dp,)), dma((n_dp,)),
           dma((n_seq,)), dma((n_seq,)), dma((n_seq,)),
           dma((3, n_seq)), dma((3, n_seq)), dma((n_dp,)), dma((n_dp,)), dma((5,))],
        compiler_params=pltpu.CompilerParams(
            collective_id=0, has_side_effects=True, vmem_limit_bytes=56 * 1024 * 1024),
        cost_estimate=pl.CostEstimate(
            flops=2 * group * width * (2 * d_out + 6 * group),
            bytes_accessed=16 * tok * all_width, transcendentals=group * group * width // HEAD_DIM),
    )(queries, keys, values, grad_out, out_weight, clip_lengths))


def solution(mesh):
    placed = (
        P(("dp", "seq"), None),
        P(("dp", "seq"), None),
        P(("dp", "seq"), None),
        P(("dp", "seq"), None),
        P("dp", "seq"),
        P("dp", None),
    )
    return jax.shard_map(
        functools.partial(body, mesh.shape["dp"], mesh.shape["seq"]),
        mesh=mesh,
        in_specs=placed,
        out_specs=(
            P(("dp", "seq"), None),
            P(("dp", "seq"), None),
            P(("dp", "seq"), None),
            P("dp", "seq"),
        ),
        check_vma=False,
    )
```
